512 devices in a mesh: aux: 32 (over x, z), occ: 16 (over y, core).
Axes of the slice: x: 4, y: 8, z: 8, core: 2. Of those that a mesh axis runs over, the one named last changes fastest.
Arguments:
- integrals: bfloat16 [12, 1024, 4096], P(None, 'aux'), may hold values from -5 to 5
- tile_pairs: int32 [32, 12, 2], P('aux'), may hold values from -1 to 15, as said below
- orbital_coef: bfloat16 [32, 16, 256], P(None, 'occ'), may hold values from -0.375 to 0.375
- domains: int32 [32, 16, 4], P(None, 'occ'), may hold values from 0 to 15, as said below
- occ_energy: bfloat16 [32, 16], P(None, 'occ'), may hold values from -1.5 to -0.29882812
- virt_energy: bfloat16 [16, 64], replicated, may hold values from 0.19921875 to 4
Outputs:
- amplitudes: bfloat16 [32, 16, 3, 1, 256, 256], P('aux', 'occ')
- pair_energy: float32 [32, 16, 3, 1], P('aux', 'occ')
The draws below stay inside these ranges and needn't reach their ends.
Inputs may be any that keep to these rules, and one draw needn't show every extreme that they name: `tile_pairs`: each owner's live slots come first and name distinct tile pairs (t1, t2) inside one block of 4 consecutive tiles; the remaining slots hold -1 in both entries. Every owner has at least (12 + 2) // 3 live slots, some owner has all 12 live, and some owner has empty slots. `domains`: each orbital's domain is 4 consecutive tiles in increasing order.
All inputs are finite; a program needn't handle non-finite values.
Results may differ from the reference program's by a relative error of at most 0.005.
Values may be sent and summed in bfloat16 or wider, within the bound.
A program may use at most 64 MiB of HBM per device.

```python
import math
import jax
import jax.numpy as jnp
from jax import lax

TILE = 64
DT = 4
NBT = 16
AUX_DEV = 32
NPT = 12
OCC_DEV = 1
STEPS = 2
AUX = 1024
OBLK = 16
NVD = 256
N_AUX = 32
N_OCC = 16


def draw_tile_pairs(key, part):
    key = jax.random.fold_in(key, 11)
    key_centre, key_order, key_live, key_full = jax.random.split(key, 4)
    owners = jnp.arange(N_AUX, dtype=jnp.int32)
    full_owner = jax.random.randint(key_full, (), 0, N_AUX, dtype=jnp.int32)
    sparse_owner = (full_owner + 1) % N_AUX
    centre = jax.random.randint(key_centre, (N_AUX,), 0, NBT - DT + 1, dtype=jnp.int32)
    centre = jnp.where(owners == full_owner, NBT - DT, centre)
    order_keys = jax.random.split(key_order, N_AUX)
    scores = jax.vmap(lambda one_key: jax.random.permutation(one_key, DT * DT))(order_keys).astype(jnp.int32)
    corner = (jnp.arange(DT * DT, dtype=jnp.int32)[None, :] == DT * DT - 1) & (owners[:, None] == full_owner)
    scores = jnp.where(corner, -1, scores)
    picked = jnp.argsort(scores, axis=1, stable=True)[:, :NPT].astype(jnp.int32)
    first = centre[:, None] + picked // DT
    second = centre[:, None] + picked % DT
    least = (NPT + 2) // 3
    live = jax.random.randint(key_live, (N_AUX,), least, NPT + 1, dtype=jnp.int32)
    live = jnp.where(owners == full_owner, NPT, live)
    live = jnp.where(owners == sparse_owner, least, live)
    valid = jnp.arange(NPT, dtype=jnp.int32)[None, :] < live[:, None]
    first = jnp.where(valid, first, -1)
    second = jnp.where(valid, second, -1)
    return jnp.stack([first, second], axis=2).astype(jnp.int32)


def draw_domains(key, part):
    key = jax.random.fold_in(key, 13)
    start = jax.random.randint(key, (N_AUX, OBLK), 0, NBT - DT + 1, dtype=jnp.int32)
    start = start.at[0, 0].set(0).at[N_AUX - 1, OBLK - 1].set(NBT - DT)
    return (start[:, :, None] + jnp.arange(DT, dtype=jnp.int32)[None, None, :]).astype(jnp.int32)


def shard_levels(stream_key, dims, cuts, low, top_value):
    factor_of = 1.0
    for dim, parts in cuts:
        heights = jax.random.uniform(jax.random.fold_in(jax.random.fold_in(stream_key, 6), dim), (parts,), jnp.float32, low / len(cuts), top_value / len(cuts))
        factor_of = factor_of * jnp.repeat(jnp.exp(heights), dims[dim] // parts).reshape((-1,) + (1,) * (len(dims) - 1 - dim))
    return factor_of


def scatter_about(key, extent, spread, reach, cuts=(), kind=jnp.bfloat16):
    result = spread * jax.random.normal(key, extent, jnp.float32)
    if cuts:
        result = result * shard_levels(key, extent, cuts, -0.22, 0.18)
    return jnp.clip(result, -reach, reach).astype(kind)


def setup_inputs(seed: int = 0) -> dict:
    seeds = jax.random.split(jax.random.key(seed), 7)
    return {
        "integrals": scatter_about(seeds[0], (NPT, AUX, TILE * TILE), 0.35, 5.0, ((1, 32),)),
        "tile_pairs": draw_tile_pairs(jax.random.fold_in(seeds[6], 71), 0),
        "orbital_coef": scatter_about(seeds[2], (N_AUX, OBLK, NVD), (DT * TILE) ** -0.5, 0.375, ((1, 16),)),
        "domains": draw_domains(jax.random.fold_in(seeds[6], 71), 0),
        "occ_energy": jnp.clip(-1.5 + 1.2011719 * jax.random.uniform(seeds[4], (N_AUX, OBLK), jnp.float32) ** shard_levels(seeds[4], (N_AUX, OBLK), ((1, 16),), -0.2, 0.2), -1.5, -0.29882812).astype(jnp.bfloat16),
        "virt_energy": jnp.clip(jnp.exp(jax.random.uniform(seeds[5], (NBT, TILE), jnp.float32, math.log(0.19921875), math.log(4.0))), 0.19921875, 4.0).astype(jnp.bfloat16),
    }


def half_transform(owner_ints, owner_pairs, coef, tiles):
    count, depth = tiles.shape
    rows = owner_ints.shape[1]
    coef_full = coef.astype(jnp.float32).reshape(count, depth, TILE)

    def slot_step(total, slot):
        block, pair = slot
        pick_first = (tiles == pair[0]).astype(jnp.float32)
        chosen = jnp.einsum('id,idm->im', pick_first, coef_full)
        block_three = block.astype(jnp.float32).reshape(rows, TILE, TILE)
        partial_y = jnp.einsum('im,pmn->pin', chosen, block_three)
        pick_second = (tiles == pair[1]).astype(jnp.float32)
        return total + jnp.einsum('id,pin->pidn', pick_second, partial_y), None

    start = jnp.zeros((rows, count, depth, TILE), jnp.float32)
    total, _ = lax.scan(slot_step, start, (owner_ints, owner_pairs))
    return total.reshape(rows, count, depth * TILE).astype(jnp.bfloat16)


def domain_energy(tiles, virt_energy):
    onehot = (tiles[..., None] == jnp.arange(virt_energy.shape[0], dtype=jnp.int32)).astype(jnp.float32)
    table = jnp.einsum('...dt,tn->...dn', onehot, virt_energy.astype(jnp.float32))
    return table.reshape(tiles.shape[:-1] + (DT * TILE,)).astype(jnp.bfloat16)


def reference(integrals, tile_pairs, orbital_coef, domains, occ_energy, virt_energy):
    owner_ints = integrals.reshape(NPT, N_AUX, AUX_DEV, TILE * TILE).transpose(1, 0, 2, 3)
    width = DT * TILE

    def block_of(row):
        coef_row = orbital_coef[row]
        tiles_row = domains[row]
        energy_row = occ_energy[row].astype(jnp.float32).reshape(N_OCC, OCC_DEV)
        halves = lax.map(lambda pieces: half_transform(pieces[0], pieces[1], coef_row, tiles_row), (owner_ints, tile_pairs))
        trans = halves.reshape(AUX, N_OCC, OCC_DEV, width).astype(jnp.float32)
        dom_row = domain_energy(tiles_row, virt_energy).astype(jnp.float32).reshape(N_OCC, OCC_DEV, width)
        amp_list = []
        energy_list = []
        for step in range(STEPS + 1):
            other = jnp.roll(trans, step, axis=1)
            other_en = jnp.roll(energy_row, step, axis=0)
            other_dom = jnp.roll(dom_row, step, axis=0)
            pair_int = jnp.einsum('poia,pojb->oijab', trans, other)
            denom = (energy_row[:, :, None, None, None] + other_en[:, None, :, None, None]
                     - dom_row[:, :, None, :, None] - other_dom[:, None, :, None, :])
            ratio = pair_int / denom
            amp_list.append(ratio.astype(jnp.bfloat16))
            energy_list.append(jnp.sum(ratio * pair_int, axis=(3, 4)) / (width * width))
        amps = jnp.stack(amp_list, axis=2).reshape(OBLK, STEPS + 1, OCC_DEV, width, width)
        pairs = jnp.stack(energy_list, axis=2).reshape(OBLK, STEPS + 1, OCC_DEV)
        return amps, pairs

    amplitudes, pair_energy = lax.map(block_of, jnp.arange(N_AUX, dtype=jnp.int32))
    return amplitudes, pair_energy
```

```python
import jax
import jax.numpy as jnp
from jax import lax
from jax.experimental import pallas as pl
from jax.experimental.pallas import tpu as pltpu
from jax.sharding import PartitionSpec as P

TILE = 64
DT = 4
NBT = 16
NPT = 12
AUX_DEV = 32
N_AUX = 32
NX = 4
NZ = 8
N_OCC = 16
WIDTH = DT * TILE
STEPS = 2
MP = TILE // 2
DEPTH = NPT * MP
HALF = 16
PARTS = AUX_DEV // HALF
GROUPS = 4
PER = N_AUX // GROUPS
MESH = pl.DeviceIdType.MESH
f32 = jnp.float32
bf16 = jnp.bfloat16


def kernel(
    ints_ref, pairs_ref, tiles_smem, coef_ref, tiles_ref, occ_ref, virt_ref,
    amp_ref, energy_ref,
    raw, rows, turned, outbox, own, next1, next2, chosen, level, level1, level2, inverse, total,
    load_sem, own_sem, send_sem, recv_sem, fwd_sem, fwd2_sem, n1_sem, n2_sem, lvl_send, lvl_recv,
):
    me = lax.axis_index("aux")
    occ = lax.axis_index("occ")
    my_x, my_z = me // NZ, me % NZ
    even = occ % 2 == 0

    def at_offset(k, sign):
        dx, dz = k // NZ, k % NZ
        return ((my_x + sign * dx + NX) % NX) * NZ + (my_z + sign * dz + NZ) % NZ

    def at_occ(step):
        return (me, (occ + step + N_OCC) % N_OCC)

    def load(part, third):
        s = third * 4
        return pltpu.make_async_copy(
            ints_ref.at[pl.ds(s, 4), pl.ds(part * HALF, HALF)],
            raw.at[pl.ds(s, 4), pl.ds(part * HALF, HALF)],
            load_sem.at[part, third],
        )

    for part in range(PARTS):
        for third in range(3):
            load(part, third).start()

    barrier = pltpu.get_barrier_semaphore()

    def greet(k, carry):
        pl.semaphore_signal(barrier, inc=1, device_id=(at_offset(k, 1), occ), device_id_type=MESH)
        return carry

    lax.fori_loop(1, N_AUX, greet, 0)
    for step in (1, 2, -1, -2):
        pl.semaphore_signal(barrier, inc=1, device_id=at_occ(step), device_id_type=MESH)

    coef = coef_ref[...]
    lane = lax.broadcasted_iota(jnp.int32, (WIDTH, 128), 1) % MP
    row = lax.broadcasted_iota(jnp.int32, (WIDTH, 128), 0)
    slot_of = lax.broadcasted_iota(jnp.int32, (1, DEPTH), 1) // MP
    first = jnp.full((1, DEPTH), -1, jnp.int32)
    second = jnp.full((1, DEPTH), -1, jnp.int32)
    for s in range(NPT):
        first = jnp.where(slot_of == s, pairs_ref[0, s, 0], first)
        second = jnp.where(slot_of == s, pairs_ref[0, s, 1], second)
    tiles = tiles_ref[...]
    for parity in range(2):
        picked = jnp.zeros((N_AUX, DEPTH), f32)
        for d in range(DT):
            spread = (row == d * TILE + 2 * lane + parity).astype(f32).astype(bf16)
            values = jnp.dot(coef, spread, preferred_element_type=f32)
            values = jnp.concatenate([values] * (DEPTH // 128), axis=1)
            picked = jnp.where(tiles[:, d : d + 1] == first, values, picked)
        for d in range(DT):
            part_rows = jnp.where(tiles[:, d : d + 1] == second, picked, 0.0)
            start = parity * 128 + (d % 2) * 64 + (d // 2) * 32
            chosen[start : start + 32, :] = part_rows.astype(bf16)

    virt = virt_ref[...].astype(f32)
    tile_row = lax.broadcasted_iota(jnp.int32, (NBT, TILE), 0)
    pieces = []
    for d in range(DT):
        mine = tiles_smem[me, 0, d]
        pieces.append(jnp.sum(jnp.where(tile_row == mine, virt, 0.0), axis=0, keepdims=True))
    domain = jnp.concatenate(pieces, axis=1)
    occ_row = lax.broadcasted_iota(jnp.int32, (N_AUX, 1), 0)
    occupied = jnp.sum(jnp.where(occ_row == me, occ_ref[...].astype(f32), 0.0), axis=0, keepdims=True)
    level[...] = jnp.broadcast_to(occupied - domain, (8, WIDTH))

    low_half = lax.broadcasted_iota(jnp.int32, (64, 128), 1) < TILE

    def transform(part):
        for third in range(3):
            load(part, third).wait()

        def spread_rows(s, carry):
            for mp in range(MP):
                base = pl.multiple_of((s * MP + mp) * HALF, HALF)
                rows[pl.ds(base, HALF), :] = raw[
                    s, part * HALF : (part + 1) * HALF, mp * 128 : (mp + 1) * 128
                ].astype(f32)
            return carry

        lax.fori_loop(0, NPT, spread_rows, 0)
        matrix = chosen[...]
        for p in range(0, HALF, 2):
            panel = jnp.concatenate(
                [rows[pl.ds(p + i, DEPTH, stride=HALF), :].astype(bf16) for i in range(2)], axis=1
            )
            product = jnp.dot(matrix, panel, preferred_element_type=f32)
            for i in range(2):
                c = slice(i * 128, (i + 1) * 128)
                straight = jnp.where(low_half, product[0:64, c], product[192:256, c])
                crossed = jnp.where(low_half, product[64:128, c], product[128:192, c])
                turned[(p + i) * 64 : (p + i + 1) * 64, :] = straight + pltpu.roll(crossed, TILE, 1)
        for r in range(N_AUX):
            for pair in range(2):
                block = turned[pl.ds(pair * 32 + r, HALF, stride=64), :]
                outbox[
                    r, part * HALF : (part + 1) * HALF, pair * 128 : (pair + 1) * 128
                ] = block.astype(bf16)

    def send(k, part):
        to = at_offset(k, -1)
        return pltpu.make_async_remote_copy(
            src_ref=outbox.at[to, pl.ds(part * HALF, HALF)],
            dst_ref=own.at[k, pl.ds(part * HALF, HALF)],
            send_sem=send_sem.at[k, part],
            recv_sem=recv_sem.at[k, part],
            device_id=(to, occ),
            device_id_type=MESH,
        )

    def start_sends(part):
        def one(k, carry):
            send(k, part).start()
            return carry

        lax.fori_loop(1, N_AUX, one, 0)

    def pass_level(step, target):
        return pltpu.make_async_remote_copy(
            src_ref=level, dst_ref=target, send_sem=lvl_send.at[step - 1], recv_sem=lvl_recv.at[step - 1],
            device_id=at_occ(step), device_id_type=MESH,
        )

    def to_next(k):
        return pltpu.make_async_remote_copy(
            src_ref=own.at[k], dst_ref=next1.at[k], send_sem=fwd_sem.at[k], recv_sem=n1_sem.at[k],
            device_id=at_occ(1), device_id_type=MESH,
        )

    def to_second(k):
        return pltpu.make_async_remote_copy(
            src_ref=own.at[k], dst_ref=next2.at[k], send_sem=fwd2_sem.at[0, k], recv_sem=n2_sem.at[k],
            device_id=at_occ(2), device_id_type=MESH,
        )

    def relay(k):
        return pltpu.make_async_remote_copy(
            src_ref=next1.at[k], dst_ref=next2.at[k], send_sem=fwd2_sem.at[1, k], recv_sem=n2_sem.at[k],
            device_id=at_occ(1), device_id_type=MESH,
        )

    def pass_on(k):
        to_next(k).start()

        @pl.when(even)
        def _():
            to_second(k).start()

    transform(0)
    pl.semaphore_wait(barrier, N_AUX - 1 + 4)
    pass_level(1, level1).start()
    pass_level(2, level2).start()
    start_sends(0)
    transform(1)
    start_sends(1)
    keep = pltpu.make_async_copy(outbox.at[me], own.at[0], own_sem)
    keep.start()

    pass_level(1, level1).wait()
    pass_level(2, level2).wait()
    column = jnp.transpose(jnp.broadcast_to(level[0:1, :], (WIDTH, WIDTH)))
    for g, other in enumerate((level, level1, level2)):
        inverse[g] = 1.0 / (column + other[0:1, :])
    keep.wait()

    def add(g, group, ref):
        k0 = group * PER
        left = own[k0 : k0 + PER].reshape(PER * AUX_DEV, WIDTH)
        right = ref[k0 : k0 + PER].reshape(PER * AUX_DEV, WIDTH)
        product = lax.dot_general(left, right, (((0,), (0,)), ((), ())), preferred_element_type=f32)
        if group == 0:
            total[g] = product
        else:
            total[g] += product

    def take_own(k, carry):
        for part in range(PARTS):
            send(k, part).wait_recv()
        pass_on(k)
        return carry

    def take_next(k, carry):
        to_next(k).wait_recv()

        @pl.when(even)
        def _():
            relay(k).start()

        return carry

    def take_second(k, carry):
        to_second(k).wait_recv()
        return carry

    pass_on(0)
    for group in range(GROUPS):
        lax.fori_loop(max(1, group * PER), (group + 1) * PER, take_own, 0)
        add(0, group, own)
        if group >= 1:
            lax.fori_loop((group - 1) * PER, group * PER, take_next, 0)
            add(1, group - 1, next1)
        if group >= 2:
            lax.fori_loop((group - 2) * PER, (group - 1) * PER, take_second, 0)
            add(2, group - 2, next2)

    def drain(k, carry):
        for part in range(PARTS):
            send(k, part).wait_send()
        return carry

    lax.fori_loop(1, N_AUX, drain, 0)
    last = GROUPS - 1
    lax.fori_loop(last * PER, N_AUX, take_next, 0)
    add(1, last, next1)
    lax.fori_loop((last - 1) * PER, last * PER, take_second, 0)
    add(2, last - 1, next2)

    def finish(g):
        value = total[g]
        ratio = value * inverse[g]
        amp_ref[g] = ratio.astype(bf16)
        energy_ref[0, g] = jnp.sum(ratio * value) / (WIDTH * WIDTH)

    finish(0)
    finish(1)

    def drain_forward(k, carry):
        to_next(k).wait_send()

        @pl.when(even)
        def _():
            to_second(k).wait_send()
            relay(k).wait_send()

        return carry

    lax.fori_loop(last * PER, N_AUX, take_second, 0)
    add(2, last, next2)
    finish(2)
    lax.fori_loop(0, N_AUX, drain_forward, 0)


def per_device(integrals, tile_pairs, orbital_coef, domains, occ_energy, virt_energy):
    vmem = pl.BlockSpec(memory_space=pltpu.VMEM)
    smem = pl.BlockSpec(memory_space=pltpu.SMEM)
    amps, energies = pl.pallas_call(
        kernel,
        out_shape=(
            jax.ShapeDtypeStruct((STEPS + 1, WIDTH, WIDTH), bf16),
            jax.ShapeDtypeStruct((1, STEPS + 1), f32),
        ),
        in_specs=[pl.BlockSpec(memory_space=pl.ANY), smem, smem, vmem, vmem, vmem, vmem],
        out_specs=(vmem, smem),
        scratch_shapes=[
            pltpu.VMEM((NPT, AUX_DEV, TILE * TILE), bf16),
            pltpu.VMEM((DEPTH * HALF, 128), f32),
            pltpu.VMEM((HALF * 64, 128), f32),
            pltpu.VMEM((N_AUX, AUX_DEV, WIDTH), bf16),
            pltpu.VMEM((N_AUX, AUX_DEV, WIDTH), bf16),
            pltpu.VMEM((N_AUX, AUX_DEV, WIDTH), bf16),
            pltpu.VMEM((N_AUX, AUX_DEV, WIDTH), bf16),
            pltpu.VMEM((256, DEPTH), bf16),
            pltpu.VMEM((8, WIDTH), f32),
            pltpu.VMEM((8, WIDTH), f32),
            pltpu.VMEM((8, WIDTH), f32),
            pltpu.VMEM((STEPS + 1, WIDTH, WIDTH), f32),
            pltpu.VMEM((STEPS + 1, WIDTH, WIDTH), f32),
            pltpu.SemaphoreType.DMA((PARTS, 3)),
            pltpu.SemaphoreType.DMA,
            pltpu.SemaphoreType.DMA((N_AUX, PARTS)),
            pltpu.SemaphoreType.DMA((N_AUX, PARTS)),
            pltpu.SemaphoreType.DMA((N_AUX,)),
            pltpu.SemaphoreType.DMA((2, N_AUX)),
            pltpu.SemaphoreType.DMA((N_AUX,)),
            pltpu.SemaphoreType.DMA((N_AUX,)),
            pltpu.SemaphoreType.DMA((2,)),
            pltpu.SemaphoreType.DMA((2,)),
        ],
        compiler_params=pltpu.CompilerParams(
            collective_id=0, has_side_effects=True, vmem_limit_bytes=40 << 20
        ),
    )(
        integrals,
        tile_pairs,
        domains,
        orbital_coef.reshape(N_AUX, WIDTH),
        domains.reshape(N_AUX, DT),
        occ_energy,
        virt_energy,
    )
    return (
        amps.reshape(1, 1, STEPS + 1, 1, WIDTH, WIDTH),
        energies.reshape(1, 1, STEPS + 1, 1),
    )


def solution(mesh):
    in_specs = (
        P(None, "aux", None),
        P("aux", None, None),
        P(None, "occ", None),
        P(None, "occ", None),
        P(None, "occ"),
        P(),
    )
    out_specs = (P("aux", "occ", None, None, None, None), P("aux", "occ", None, None))
    return jax.shard_map(
        per_device, mesh=mesh, in_specs=in_specs, out_specs=out_specs, check_vma=False
    )
```

```python
import jax
import jax.numpy as jnp
from jax import lax
from jax.experimental import pallas as pl
from jax.experimental.pallas import tpu as pltpu
from jax.sharding import PartitionSpec as P

TILE = 64
DT = 4
NBT = 16
NPT = 12
AUX_DEV = 32
N_AUX = 32
NX = 4
NZ = 8
N_OCC = 16
WIDTH = DT * TILE
STEPS = 2
MP = TILE // 2
DEPTH = NPT * MP
HALF = 16
PARTS = AUX_DEV // HALF
BUNCH = 4
BUNCHES = N_AUX // BUNCH
LAG = 4
MESH = pl.DeviceIdType.MESH
f32 = jnp.float32
bf16 = jnp.bfloat16


def kernel(
    ints_ref, pairs_hbm, coef_hbm, tiles_hbm, occ_hbm, virt_hbm,
    amp_ref, energy_ref,
    pairs_ref, coef_ref, tiles_ref, occ_ref, virt_ref,
    raw, rows, turned, outbox, own, next1, next2, chosen, level, level1, level2, inverse, total,
    small_sem, load_sem, own_sem, send_sem, recv_sem, fwd_sem, n1_sem, n2_sem, lvl_send, lvl_recv,
):
    me = lax.axis_index("aux")
    occ = lax.axis_index("occ")
    my_x, my_z = me // NZ, me % NZ
    even = occ % 2 == 0

    x_at = [lax.rem(my_x + NX - dx, NX) * NZ for dx in range(NX)]
    z_at = [lax.rem(my_z + NZ - dz, NZ) for dz in range(NZ)]

    def behind(k):
        return x_at[k // NZ] + z_at[k % NZ]

    def at_occ(step):
        return (me, (occ + step + N_OCC) % N_OCC)

    barrier = pltpu.get_barrier_semaphore()

    for k in range(1, N_AUX):
        pl.semaphore_signal(barrier, inc=1, device_id=(behind(k), occ), device_id_type=MESH)
    for step in (1, 2, -1, -2):
        pl.semaphore_signal(barrier, inc=1, device_id=at_occ(step), device_id_type=MESH)

    def load(part, third):
        s = third * 4
        return pltpu.make_async_copy(
            ints_ref.at[pl.ds(s, 4), pl.ds(part * HALF, HALF)],
            raw.at[pl.ds(s, 4), pl.ds(part * HALF, HALF)],
            load_sem.at[part, third],
        )

    small = [
        pltpu.make_async_copy(src, dst, small_sem.at[i])
        for i, (src, dst) in enumerate((
            (coef_hbm, coef_ref), (tiles_hbm, tiles_ref), (pairs_hbm, pairs_ref),
            (occ_hbm, occ_ref), (virt_hbm, virt_ref),
        ))
    ]
    for copy in small:
        copy.start()
    for part in range(PARTS):
        for third in range(3):
            load(part, third).start()

    for copy in small:
        copy.wait()

    coef = coef_ref[...]
    lane = lax.broadcasted_iota(jnp.int32, (WIDTH, 128), 1) % MP
    row = lax.broadcasted_iota(jnp.int32, (WIDTH, 128), 0)
    slot_of = lax.broadcasted_iota(jnp.int32, (1, DEPTH), 1) // MP
    pairs = pairs_ref[...]
    first = jnp.full((1, DEPTH), -1, jnp.int32)
    second = jnp.full((1, DEPTH), -1, jnp.int32)
    for s in range(NPT):
        first = jnp.where(slot_of == s, pairs[0:1, s : s + 1], first)
        second = jnp.where(slot_of == s, pairs[1:2, s : s + 1], second)
    tiles = tiles_ref[...]
    diagonal = lax.broadcasted_iota(jnp.int32, (N_AUX, N_AUX), 0) == lax.broadcasted_iota(
        jnp.int32, (N_AUX, N_AUX), 1
    )
    tile_of = [
        jnp.sum(jnp.where(diagonal, tiles[d : d + 1, :], 0), axis=1, keepdims=True) for d in range(DT)
    ]
    for parity in range(2):
        picked = jnp.zeros((N_AUX, DEPTH), f32)
        for d in range(DT):
            spread = (row == d * TILE + 2 * lane + parity).astype(f32).astype(bf16)
            values = jnp.dot(coef, spread, preferred_element_type=f32)
            values = jnp.concatenate([values] * (DEPTH // 128), axis=1)
            picked = jnp.where(tile_of[d] == first, values, picked)
        for d in range(DT):
            part_rows = jnp.where(tile_of[d] == second, picked, 0.0)
            start = parity * 128 + (d % 2) * 64 + (d // 2) * 32
            chosen[start : start + 32, :] = part_rows.astype(bf16)

    virt = virt_ref[...].astype(f32)
    tile_row = lax.broadcasted_iota(jnp.int32, (NBT, TILE), 0)
    mine = lax.broadcasted_iota(jnp.int32, (1, N_AUX), 1) == me
    pieces = []
    for d in range(DT):
        tile = jnp.sum(jnp.where(mine, tiles[d : d + 1, :], 0), axis=1, keepdims=True)
        pieces.append(jnp.sum(jnp.where(tile_row == tile, virt, 0.0), axis=0, keepdims=True))
    domain = jnp.concatenate(pieces, axis=1)
    occupied = jnp.sum(jnp.where(mine, occ_ref[...].astype(f32), 0.0), axis=1, keepdims=True)
    level[...] = jnp.broadcast_to(occupied - domain, (8, WIDTH))

    low_half = lax.broadcasted_iota(jnp.int32, (64, 128), 1) < TILE

    def transform(part):
        for third in range(3):
            load(part, third).wait()

        def spread_rows(s, carry):
            for mp in range(MP):
                base = pl.multiple_of((s * MP + mp) * HALF, HALF)
                rows[pl.ds(base, HALF), :] = raw[
                    s, part * HALF : (part + 1) * HALF, mp * 128 : (mp + 1) * 128
                ].astype(f32)
            return carry

        lax.fori_loop(0, NPT, spread_rows, 0)
        matrix = chosen[...]
        for p in range(0, HALF, 2):
            panel = jnp.concatenate(
                [rows[pl.ds(p + i, DEPTH, stride=HALF), :].astype(bf16) for i in range(2)], axis=1
            )
            product = jnp.dot(matrix, panel, preferred_element_type=f32)
            for i in range(2):
                c = slice(i * 128, (i + 1) * 128)
                straight = jnp.where(low_half, product[0:64, c], product[192:256, c])
                crossed = jnp.where(low_half, product[64:128, c], product[128:192, c])
                turned[(p + i) * 64 : (p + i + 1) * 64, :] = straight + pltpu.roll(crossed, TILE, 1)
        for r in range(N_AUX):
            for pair in range(2):
                block = turned[pl.ds(pair * 32 + r, HALF, stride=64), :]
                outbox[
                    r, part * HALF : (part + 1) * HALF, pair * 128 : (pair + 1) * 128
                ] = block.astype(bf16)

    def start_sends(part):
        for k in range(1, N_AUX):
            to = behind(k)
            pltpu.make_async_remote_copy(
                src_ref=outbox.at[to, pl.ds(part * HALF, HALF)],
                dst_ref=own.at[part, k],
                send_sem=send_sem,
                recv_sem=recv_sem.at[part, k // BUNCH],
                device_id=(to, occ),
                device_id_type=MESH,
            ).start()

    def pass_level(step, target):
        return pltpu.make_async_remote_copy(
            src_ref=level, dst_ref=target, send_sem=lvl_send.at[step - 1], recv_sem=lvl_recv.at[step - 1],
            device_id=at_occ(step), device_id_type=MESH,
        )

    def bunch(ref, i):
        part, j = i // BUNCHES, i % BUNCHES
        return ref.at[part, pl.ds(j * BUNCH, BUNCH)]

    def to_next(i):
        return pltpu.make_async_remote_copy(
            src_ref=bunch(own, i), dst_ref=bunch(next1, i), send_sem=fwd_sem.at[0], recv_sem=n1_sem.at[i],
            device_id=at_occ(1), device_id_type=MESH,
        )

    def to_second(i):
        return pltpu.make_async_remote_copy(
            src_ref=bunch(own, i), dst_ref=bunch(next2, i), send_sem=fwd_sem.at[1], recv_sem=n2_sem.at[i],
            device_id=at_occ(2), device_id_type=MESH,
        )

    def relay(i):
        return pltpu.make_async_remote_copy(
            src_ref=bunch(next1, i), dst_ref=bunch(next2, i), send_sem=fwd_sem.at[2], recv_sem=n2_sem.at[i],
            device_id=at_occ(1), device_id_type=MESH,
        )

    def whole(index):
        return pltpu.make_async_remote_copy(
            src_ref=own, dst_ref=next1, send_sem=fwd_sem.at[index], recv_sem=n1_sem.at[0],
            device_id=at_occ(1), device_id_type=MESH,
        )

    def take_own(i):
        part, j = i // BUNCHES, i % BUNCHES
        k0 = max(1, j * BUNCH)
        came = own.at[part, pl.ds(k0, (j + 1) * BUNCH - k0)]
        pltpu.make_async_remote_copy(
            src_ref=came, dst_ref=came, send_sem=send_sem, recv_sem=recv_sem.at[part, j],
            device_id=at_occ(1), device_id_type=MESH,
        ).wait_recv()
        to_next(i).start()

        @pl.when(even)
        def _():
            to_second(i).start()

    def take_next(i):
        to_next(i).wait_recv()

        @pl.when(even)
        def _():
            relay(i).start()

    def take_second(i):
        to_second(i).wait_recv()

    early = my_z < NZ // 2
    transform(0)

    @pl.when(early)
    def _():
        transform(1)

    pl.semaphore_wait(barrier, N_AUX - 1 + 4)
    pass_level(1, level1).start()
    pass_level(2, level2).start()
    start_sends(0)

    @pl.when(jnp.logical_not(early))
    def _():
        transform(1)

    start_sends(1)
    keep = [pltpu.make_async_copy(outbox.at[me, pl.ds(part * HALF, HALF)], own.at[part, 0], own_sem.at[part]) for part in range(PARTS)]
    for copy in keep:
        copy.start()
    for copy in keep:
        copy.wait()
    pass_level(1, level1).wait()
    pass_level(2, level2).wait()
    column = jnp.transpose(jnp.broadcast_to(level[0:1, :], (WIDTH, WIDTH)))
    for g, other in enumerate((level, level1, level2)):
        inverse[g] = 1.0 / (column + other[0:1, :])

    def add(g, group, ref):
        part, k0 = group // 2, group % 2 * 16
        left = own[part, k0 : k0 + 16].reshape(WIDTH, WIDTH)
        right = ref[part, k0 : k0 + 16].reshape(WIDTH, WIDTH)
        product = lax.dot_general(left, right, (((0,), (0,)), ((), ())), preferred_element_type=f32)
        if group == 0:
            total[g] = product
        else:
            total[g] += product

    per_group = 2 * BUNCHES // 4

    for i in range(2 * BUNCHES):
        take_own(i)
        if i >= LAG:
            take_next(i - LAG)
        if i >= 2 * LAG:
            take_second(i - 2 * LAG)
        done = i + 1
        if done % per_group == 0:
            add(0, done // per_group - 1, own)
        done = i + 1 - LAG
        if done > 0 and done % per_group == 0:
            add(1, done // per_group - 1, next1)
        done = i + 1 - 2 * LAG
        if done > 0 and done % per_group == 0:
            add(2, done // per_group - 1, next2)
    for i in range(2 * BUNCHES - LAG, 2 * BUNCHES):
        take_next(i)
    for i in range(2 * BUNCHES - LAG, 2 * BUNCHES):
        done = i + 1
        if done % per_group == 0:
            add(1, done // per_group - 1, next1)

    def finish(g):
        value = total[g]
        ratio = value * inverse[g]
        amp_ref[g] = ratio.astype(bf16)
        energy_ref[0, g] = jnp.sum(ratio * value) / (WIDTH * WIDTH)

    finish(0)
    finish(1)
    for i in range(2 * BUNCHES - 2 * LAG, 2 * BUNCHES):
        take_second(i)
        done = i + 1
        if done % per_group == 0:
            add(2, done // per_group - 1, next2)
    finish(2)
    sent = outbox.at[pl.ds(0, N_AUX - 1)]
    pltpu.make_async_remote_copy(
        src_ref=sent, dst_ref=sent, send_sem=send_sem, recv_sem=recv_sem.at[0, 0],
        device_id=at_occ(1), device_id_type=MESH,
    ).wait_send()
    whole(0).wait_send()

    @pl.when(even)
    def _():
        whole(1).wait_send()
        whole(2).wait_send()


def per_device(integrals, tile_pairs, orbital_coef, domains, occ_energy, virt_energy):
    vmem = pl.BlockSpec(memory_space=pltpu.VMEM)
    smem = pl.BlockSpec(memory_space=pltpu.SMEM)
    amps, energies = pl.pallas_call(
        kernel,
        out_shape=(
            jax.ShapeDtypeStruct((STEPS + 1, WIDTH, WIDTH), bf16),
            jax.ShapeDtypeStruct((1, STEPS + 1), f32),
        ),
        in_specs=[pl.BlockSpec(memory_space=pltpu.HBM)] * 6,
        out_specs=(vmem, smem),
        scratch_shapes=[
            pltpu.VMEM((2, NPT), jnp.int32),
            pltpu.VMEM((N_AUX, WIDTH), bf16),
            pltpu.VMEM((DT, N_AUX), jnp.int32),
            pltpu.VMEM((1, N_AUX), bf16),
            pltpu.VMEM((NBT, TILE), bf16),
            pltpu.VMEM((NPT, AUX_DEV, TILE * TILE), bf16),
            pltpu.VMEM((DEPTH * HALF, 128), f32),
            pltpu.VMEM((HALF * 64, 128), f32),
            pltpu.VMEM((N_AUX, AUX_DEV, WIDTH), bf16),
            pltpu.VMEM((PARTS, N_AUX, HALF, WIDTH), bf16),
            pltpu.VMEM((PARTS, N_AUX, HALF, WIDTH), bf16),
            pltpu.VMEM((PARTS, N_AUX, HALF, WIDTH), bf16),
            pltpu.VMEM((256, DEPTH), bf16),
            pltpu.VMEM((8, WIDTH), f32),
            pltpu.VMEM((8, WIDTH), f32),
            pltpu.VMEM((8, WIDTH), f32),
            pltpu.VMEM((STEPS + 1, WIDTH, WIDTH), f32),
            pltpu.VMEM((STEPS + 1, WIDTH, WIDTH), f32),
            pltpu.SemaphoreType.DMA((5,)),
            pltpu.SemaphoreType.DMA((PARTS, 3)),
            pltpu.SemaphoreType.DMA((PARTS,)),
            pltpu.SemaphoreType.DMA,
            pltpu.SemaphoreType.DMA((PARTS, BUNCHES)),
            pltpu.SemaphoreType.DMA((3,)),
            pltpu.SemaphoreType.DMA((PARTS * BUNCHES,)),
            pltpu.SemaphoreType.DMA((PARTS * BUNCHES,)),
            pltpu.SemaphoreType.DMA((2,)),
            pltpu.SemaphoreType.DMA((2,)),
        ],
        compiler_params=pltpu.CompilerParams(
            collective_id=0, has_side_effects=True, vmem_limit_bytes=40 << 20
        ),
    )(
        *[
            pltpu.with_memory_space_constraint(value, pltpu.HBM)
            for value in (
                integrals,
                tile_pairs.reshape(NPT, 2).T,
                orbital_coef.reshape(N_AUX, WIDTH),
                domains.reshape(N_AUX, DT).T,
                occ_energy.T,
                virt_energy,
            )
        ]
    )
    return (
        amps.reshape(1, 1, STEPS + 1, 1, WIDTH, WIDTH),
        energies.reshape(1, 1, STEPS + 1, 1),
    )


def solution(mesh):
    in_specs = (
        P(None, "aux", None),
        P("aux", None, None),
        P(None, "occ", None),
        P(None, "occ", None),
        P(None, "occ"),
        P(),
    )
    out_specs = (P("aux", "occ", None, None, None, None), P("aux", "occ", None, None))
    return jax.shard_map(
        per_device, mesh=mesh, in_specs=in_specs, out_specs=out_specs, check_vma=False
    )
```

```python
import jax
import jax.numpy as jnp
from jax import lax
from jax.experimental import pallas as pl
from jax.experimental.pallas import tpu as pltpu
from jax.sharding import PartitionSpec as P

TILE = 64
DT = 4
NBT = 16
NPT = 12
AUX_DEV = 32
N_AUX = 32
NX = 4
NZ = 8
N_OCC = 16
WIDTH = DT * TILE
STEPS = 2
MP = TILE // 2
DEPTH = NPT * MP
HALF = 16
PARTS = AUX_DEV // HALF
SIDE = 16
BUNCH = 4
BUNCHES = [(0, 0, j) for j in range(0, SIDE, BUNCH)]
BUNCHES += [(1, part, j) for part in range(PARTS) for j in range(0, SIDE, BUNCH)]
N_FIRST = SIDE // BUNCH
N_BUNCH = len(BUNCHES)
ANSWER = 1
PACE = 2
AHEAD = 8
LAG = 3
LAG2 = 5
OFFSETS = [(dx, dz) for dx in range(NX) for dz in range(NZ // 2)]
EARLY = (tuple(range(N_BUNCH)), (10, 11))
LATE = (tuple(range(N_FIRST, N_BUNCH)) + tuple(range(N_FIRST)), ())
PITCH = 20
TURN = 72
MESH = pl.DeviceIdType.MESH
f32 = jnp.float32
bf16 = jnp.bfloat16


def kernel(
    ints_ref, pairs_hbm, coef_hbm, tiles_hbm, occ_hbm, virt_hbm,
    amp_ref, energy_ref,
    pairs_ref, coef_ref, tiles_ref, occ_ref, virt_ref,
    raw, rows, turned, outbox, own_a, own_b, next1_a, next1_b, next2_a, next2_b, chosen, level, level1, level2, inverse, total,
    small_sem, load_sem, late_sem, send_sem, recv_sem, fwd_sem, n1_sem, n2_sem, lvl_send, lvl_recv,
):
    me = lax.axis_index("aux")
    occ = lax.axis_index("occ")
    my_x, my_z = me // NZ, me % NZ
    even = occ % 2 == 0

    early = my_z < NZ // 2
    late = jnp.logical_not(early)
    x_at = [lax.rem(my_x + NX - dx, NX) * NZ for dx in range(NX)]
    z_at = [lax.rem(my_z + NZ - dz, NZ // 2) for dz in range(NZ // 2)]

    def behind(side, j):
        dx, dz = OFFSETS[j]
        return x_at[dx] + side * (NZ // 2) + z_at[dz]

    def at_occ(step):
        return (me, (occ + step + N_OCC) % N_OCC)

    barrier = pltpu.get_barrier_semaphore()

    def greet(side, start):
        for j in range(start, SIDE):
            pl.semaphore_signal(barrier, inc=1, device_id=(behind(side, j), occ), device_id_type=MESH)

    @pl.when(early)
    def _():
        greet(0, 1)
        greet(1, 0)

    @pl.when(late)
    def _():
        greet(1, 1)

    for step in (1, 2, -1, -2):
        pl.semaphore_signal(barrier, inc=1, device_id=at_occ(step), device_id_type=MESH)

    def load(part, third):
        s = third * 4
        return pltpu.make_async_copy(
            ints_ref.at[pl.ds(s, 4), pl.ds(part * HALF, HALF)],
            raw.at[pl.ds(s, 4), pl.ds(part * HALF, HALF)],
            load_sem.at[part, third],
        )

    small = [
        pltpu.make_async_copy(src, dst, small_sem.at[i])
        for i, (src, dst) in enumerate((
            (coef_hbm, coef_ref), (tiles_hbm, tiles_ref), (pairs_hbm, pairs_ref),
            (occ_hbm, occ_ref), (virt_hbm, virt_ref),
        ))
    ]
    for copy in small:
        copy.start()
    for part in range(PARTS):
        for third in range(3):
            load(part, third).start()

    for copy in small:
        copy.wait()

    coef = coef_ref[...]
    lane = lax.broadcasted_iota(jnp.int32, (WIDTH, 128), 1) % MP
    row = lax.broadcasted_iota(jnp.int32, (WIDTH, 128), 0)
    slot_of = lax.broadcasted_iota(jnp.int32, (1, DEPTH), 1) // MP
    pairs = pairs_ref[...]
    first = jnp.full((1, DEPTH), -1, jnp.int32)
    second = jnp.full((1, DEPTH), -1, jnp.int32)
    for s in range(NPT):
        first = jnp.where(slot_of == s, pairs[0:1, s : s + 1], first)
        second = jnp.where(slot_of == s, pairs[1:2, s : s + 1], second)
    tiles = tiles_ref[...]
    diagonal = lax.broadcasted_iota(jnp.int32, (N_AUX, N_AUX), 0) == lax.broadcasted_iota(
        jnp.int32, (N_AUX, N_AUX), 1
    )
    tile_of = [
        jnp.sum(jnp.where(diagonal, tiles[d : d + 1, :], 0), axis=1, keepdims=True) for d in range(DT)
    ]
    for parity in range(2):
        picked = jnp.zeros((N_AUX, DEPTH), f32)
        for d in range(DT):
            spread = (row == d * TILE + 2 * lane + parity).astype(f32).astype(bf16)
            values = jnp.dot(coef, spread, preferred_element_type=f32)
            values = jnp.concatenate([values] * (DEPTH // 128), axis=1)
            picked = jnp.where(tile_of[d] == first, values, picked)
        for d in range(DT):
            part_rows = jnp.where(tile_of[d] == second, picked, 0.0)
            start = parity * 128 + (d % 2) * 64 + (d // 2) * 32
            chosen[start : start + 32, :] = part_rows.astype(bf16)

    virt = virt_ref[...].astype(f32)
    tile_row = lax.broadcasted_iota(jnp.int32, (NBT, TILE), 0)
    mine = lax.broadcasted_iota(jnp.int32, (1, N_AUX), 1) == me
    pieces = []
    for d in range(DT):
        tile = jnp.sum(jnp.where(mine, tiles[d : d + 1, :], 0), axis=1, keepdims=True)
        pieces.append(jnp.sum(jnp.where(tile_row == tile, virt, 0.0), axis=0, keepdims=True))
    domain = jnp.concatenate(pieces, axis=1)
    occupied = jnp.sum(jnp.where(mine, occ_ref[...].astype(f32), 0.0), axis=1, keepdims=True)
    level[...] = jnp.broadcast_to(occupied - domain, (8, WIDTH))

    low_half = lax.broadcasted_iota(jnp.int32, (64, 128), 1) < TILE

    def transform(part):
        for third in range(3):
            load(part, third).wait()

        def spread_rows(s, carry):
            for mp in range(MP):
                base = (s * MP + mp) * PITCH
                rows[pl.ds(base, HALF), :] = raw[
                    s, part * HALF : (part + 1) * HALF, mp * 128 : (mp + 1) * 128
                ].astype(f32)
            return carry

        lax.fori_loop(0, NPT, spread_rows, 0)
        matrix = chosen[...]
        for p in range(0, HALF, 2):
            panel = jnp.concatenate(
                [rows[pl.ds(p + i, DEPTH, stride=PITCH), :].astype(bf16) for i in range(2)], axis=1
            )
            product = jnp.dot(matrix, panel, preferred_element_type=f32)
            for i in range(2):
                c = slice(i * 128, (i + 1) * 128)
                straight = jnp.where(low_half, product[0:64, c], product[192:256, c])
                crossed = jnp.where(low_half, product[64:128, c], product[128:192, c])
                turned[(p + i) * TURN : (p + i) * TURN + 64, :] = straight + pltpu.roll(crossed, TILE, 1)
        for r in range(N_AUX):
            for pair in range(2):
                block = turned[pl.ds(pair * 32 + r, HALF, stride=TURN), :]
                outbox[
                    r, part * HALF : (part + 1) * HALF, pair * 128 : (pair + 1) * 128
                ] = block.astype(bf16)

    def send(side, same, part, js=range(SIDE)):
        for j in js:
            to = behind(side, j)
            if part is None:
                src, dst, sem = outbox.at[to], own_a.at[j], recv_sem.at[j // BUNCH]
            else:
                src, dst = outbox.at[to, pl.ds(part * HALF, HALF)], own_b.at[part, j]
                sem = recv_sem.at[N_FIRST * (1 + part) + j // BUNCH]
            if same and j == 0:
                pltpu.make_async_copy(src, dst, sem).start()
            else:
                pltpu.make_async_remote_copy(
                    src_ref=src, dst_ref=dst, send_sem=send_sem, recv_sem=sem,
                    device_id=(to, occ), device_id_type=MESH,
                ).start()

    def pass_level(step, target):
        return pltpu.make_async_remote_copy(
            src_ref=level, dst_ref=target, send_sem=lvl_send.at[step - 1], recv_sem=lvl_recv.at[step - 1],
            device_id=at_occ(step), device_id_type=MESH,
        )

    own, next1, next2 = (own_a, own_b), (next1_a, next1_b), (next2_a, next2_b)

    def bunch(refs, i):
        which, part, j = BUNCHES[i]
        if which == 0:
            return refs[0].at[pl.ds(j, BUNCH)]
        return refs[1].at[part, pl.ds(j, BUNCH)]

    def to_next(i):
        return pltpu.make_async_remote_copy(
            src_ref=bunch(own, i), dst_ref=bunch(next1, i), send_sem=fwd_sem.at[0], recv_sem=n1_sem.at[i],
            device_id=at_occ(1), device_id_type=MESH,
        )

    def to_second(i):
        return pltpu.make_async_remote_copy(
            src_ref=bunch(own, i), dst_ref=bunch(next2, i), send_sem=fwd_sem.at[1], recv_sem=n2_sem.at[i],
            device_id=at_occ(2), device_id_type=MESH,
        )

    def relay(i):
        return pltpu.make_async_remote_copy(
            src_ref=bunch(next1, i), dst_ref=bunch(next2, i), send_sem=fwd_sem.at[2], recv_sem=n2_sem.at[i],
            device_id=at_occ(1), device_id_type=MESH,
        )

    def drain(ref, sem):
        pltpu.make_async_remote_copy(
            src_ref=ref, dst_ref=ref, send_sem=sem, recv_sem=recv_sem.at[0],
            device_id=at_occ(1), device_id_type=MESH,
        ).wait_send()

    def take_own(i, direct):
        came = bunch(own, i)
        pltpu.make_async_remote_copy(
            src_ref=came, dst_ref=came, send_sem=send_sem, recv_sem=recv_sem.at[i],
            device_id=at_occ(1), device_id_type=MESH,
        ).wait_recv()
        if i in direct:
            to_second(i).start()
        else:

            @pl.when(even)
            def _():
                to_second(i).start()

        to_next(i).start()

    def take_next(i, direct):
        to_next(i).wait_recv()
        if i not in direct:

            @pl.when(even)
            def _():
                relay(i).start()

    def take_second(i):
        to_second(i).wait_recv()

    def send_late(i):
        part, first_j = divmod(i * BUNCH, SIDE)
        send(1, True, part, range(first_j, first_j + BUNCH))

    transform(0)

    @pl.when(early)
    def _():
        transform(1)

    pl.semaphore_wait(barrier, jnp.where(early, SIDE - 1 + 4, N_AUX - 1 + 4))

    @pl.when(early)
    def _():
        send(0, True, None)

    @pl.when(late)
    def _():
        for j in range(SIDE):
            pl.semaphore_signal(late_sem, inc=1, device_id=(behind(0, j), occ), device_id_type=MESH)
        send(0, False, 0)
        transform(1)
        send(0, False, 1)
        for i in range(AHEAD):
            send_late(i)

    pass_level(1, level1).start()
    pass_level(2, level2).start()

    def multiply(g, refs, which, part, fresh):
        left, right = own[which], refs[which]
        if which == 0:
            left, right = left[...], right[...]
        else:
            left, right = left[part], right[part]
        depth = left.shape[0] * left.shape[1]
        product = lax.dot_general(
            left.reshape(depth, WIDTH), right.reshape(depth, WIDTH),
            (((0,), (0,)), ((), ())), preferred_element_type=f32,
        )
        total[g] = product if fresh else total[g] + product

    def finish(g):
        value = total[g]
        ratio = value * inverse[g]
        amp_ref[g] = ratio.astype(bf16)
        energy_ref[0, g] = jnp.sum(ratio * value) / (WIDTH * WIDTH)

    def energies():
        pass_level(1, level1).wait()
        pass_level(2, level2).wait()
        column = jnp.transpose(jnp.broadcast_to(level[0:1, :], (WIDTH, WIDTH)))
        for g, other in enumerate((level, level1, level2)):
            inverse[g] = 1.0 / (column + other[0:1, :])

    def pipeline(order, direct, hook):
        count = {}

        def advance(g, refs, i):
            which, part, _ = BUNCHES[i]
            key = (g, which, part)
            count[key] = count.get(key, 0) + 1
            if count[key] == N_FIRST:
                fresh = not any(k[0] == g and k != key and n == N_FIRST for k, n in count.items())
                multiply(g, refs, which, part, fresh)

        n = N_BUNCH
        for step in range(n):
            take_own(order[step], direct)
            hook(step)
            if step >= LAG:
                take_next(order[step - LAG], direct)
            if step >= LAG2:
                take_second(order[step - LAG2])
            if step == n - 1:
                for back in range(LAG - 1, 0, -1):
                    take_next(order[n - 1 - back], direct)
            advance(0, own, order[step])
            if step >= LAG:
                advance(1, next1, order[step - LAG])
            if step >= LAG2:
                advance(2, next2, order[step - LAG2])
            if step == LAG2:
                energies()
        finish(0)
        take_next(order[n - 1], direct)
        for back in range(LAG - 1, -1, -1):
            advance(1, next1, order[n - 1 - back])
        finish(1)
        for back in range(LAG2 - 1, -1, -1):
            take_second(order[n - 1 - back])
            advance(2, next2, order[n - 1 - back])
        finish(2)
        drain(outbox.at[pl.ds(0, N_AUX - 1)], send_sem)
        drain(own_a, fwd_sem.at[0])
        drain(own_b, fwd_sem.at[0])

        @pl.when(even)
        def _():
            drain(own_a, fwd_sem.at[1])
            drain(own_b, fwd_sem.at[1])
            for i in order:
                if i not in direct:
                    drain(bunch(own, i), fwd_sem.at[2])

        @pl.when(jnp.logical_not(even))
        def _():
            for i in direct:
                drain(bunch(own, i), fwd_sem.at[1])

    @pl.when(early)
    def _():
        def hook(step):
            if step == ANSWER:
                pl.semaphore_wait(late_sem, SIDE)
            start = (step - ANSWER) * PACE
            if 0 <= start < SIDE:
                send(1, False, None, range(start, start + PACE))

        pipeline(*EARLY, hook)

    @pl.when(late)
    def _():
        def hook(step):
            if step + AHEAD < PARTS * N_FIRST:
                send_late(step + AHEAD)

        pipeline(*LATE, hook)


def per_device(integrals, tile_pairs, orbital_coef, domains, occ_energy, virt_energy):
    vmem = pl.BlockSpec(memory_space=pltpu.VMEM)
    smem = pl.BlockSpec(memory_space=pltpu.SMEM)
    amps, energies = pl.pallas_call(
        kernel,
        out_shape=(
            jax.ShapeDtypeStruct((STEPS + 1, WIDTH, WIDTH), bf16),
            jax.ShapeDtypeStruct((1, STEPS + 1), f32),
        ),
        in_specs=[pl.BlockSpec(memory_space=pltpu.HBM)] * 6,
        out_specs=(vmem, smem),
        scratch_shapes=[
            pltpu.VMEM((2, NPT), jnp.int32),
            pltpu.VMEM((N_AUX, WIDTH), bf16),
            pltpu.VMEM((DT, N_AUX), jnp.int32),
            pltpu.VMEM((1, N_AUX), bf16),
            pltpu.VMEM((NBT, TILE), bf16),
            pltpu.VMEM((NPT, AUX_DEV, TILE * TILE), bf16),
            pltpu.VMEM((DEPTH * PITCH, 128), f32),
            pltpu.VMEM((HALF * TURN, 128), f32),
            pltpu.VMEM((N_AUX, AUX_DEV, WIDTH), bf16),
            pltpu.VMEM((SIDE, AUX_DEV, WIDTH), bf16),
            pltpu.VMEM((PARTS, SIDE, HALF, WIDTH), bf16),
            pltpu.VMEM((SIDE, AUX_DEV, WIDTH), bf16),
            pltpu.VMEM((PARTS, SIDE, HALF, WIDTH), bf16),
            pltpu.VMEM((SIDE, AUX_DEV, WIDTH), bf16),
            pltpu.VMEM((PARTS, SIDE, HALF, WIDTH), bf16),
            pltpu.VMEM((256, DEPTH), bf16),
            pltpu.VMEM((8, WIDTH), f32),
            pltpu.VMEM((8, WIDTH), f32),
            pltpu.VMEM((8, WIDTH), f32),
            pltpu.VMEM((STEPS + 1, WIDTH, WIDTH), f32),
            pltpu.VMEM((STEPS + 1, WIDTH, WIDTH), f32),
            pltpu.SemaphoreType.DMA((5,)),
            pltpu.SemaphoreType.DMA((PARTS, 3)),
            pltpu.SemaphoreType.REGULAR,
            pltpu.SemaphoreType.DMA,
            pltpu.SemaphoreType.DMA((N_BUNCH,)),
            pltpu.SemaphoreType.DMA((3,)),
            pltpu.SemaphoreType.DMA((N_BUNCH,)),
            pltpu.SemaphoreType.DMA((N_BUNCH,)),
            pltpu.SemaphoreType.DMA((2,)),
            pltpu.SemaphoreType.DMA((2,)),
        ],
        compiler_params=pltpu.CompilerParams(
            collective_id=0, has_side_effects=True, vmem_limit_bytes=40 << 20
        ),
    )(
        *[
            pltpu.with_memory_space_constraint(value, pltpu.HBM)
            for value in (
                integrals,
                tile_pairs.reshape(NPT, 2).T,
                orbital_coef.reshape(N_AUX, WIDTH),
                domains.reshape(N_AUX, DT).T,
                occ_energy.T,
                virt_energy,
            )
        ]
    )
    return (
        amps.reshape(1, 1, STEPS + 1, 1, WIDTH, WIDTH),
        energies.reshape(1, 1, STEPS + 1, 1),
    )


def solution(mesh):
    in_specs = (
        P(None, "aux", None),
        P("aux", None, None),
        P(None, "occ", None),
        P(None, "occ", None),
        P(None, "occ"),
        P(),
    )
    out_specs = (P("aux", "occ", None, None, None, None), P("aux", "occ", None, None))
    return jax.shard_map(
        per_device, mesh=mesh, in_specs=in_specs, out_specs=out_specs, check_vma=False
    )
```

```python
import jax
import jax.numpy as jnp
from jax import lax
from jax.experimental import pallas as pl
from jax.experimental.pallas import tpu as pltpu
from jax.sharding import PartitionSpec as P

TILE = 64
DT = 4
NBT = 16
NPT = 12
AUX_DEV = 32
N_AUX = 32
NX = 4
NZ = 8
N_OCC = 16
WIDTH = DT * TILE
STEPS = 2
MP = TILE // 2
DEPTH = NPT * MP
HALF = 16
PARTS = AUX_DEV // HALF
SIDE = 16
BUNCH = 4
BUNCHES = [(0, 0, j) for j in range(0, SIDE, BUNCH)]
BUNCHES += [(1, part, j) for part in range(PARTS) for j in range(0, SIDE, BUNCH)]
N_FIRST = SIDE // BUNCH
N_BUNCH = len(BUNCHES)
ANSWER = 1
PACE = 2
AHEAD = 8
LAG = 3
LAG2 = 5
OFFSETS = [(dx, dz) for dx in range(NX) for dz in range(NZ // 2)]
EARLY = (tuple(range(N_BUNCH)), (10, 11))
LATE = (tuple(range(N_FIRST, N_BUNCH)) + tuple(range(N_FIRST)), ())
PITCH = 20
TURN = 72
MESH = pl.DeviceIdType.MESH
f32 = jnp.float32
bf16 = jnp.bfloat16


def kernel(
    ints_ref, pairs_hbm, coef_hbm, tiles_hbm, occ_hbm, virt_hbm,
    amp_ref, energy_ref,
    pairs_ref, coef_ref, tiles_ref, occ_ref, virt_ref,
    raw, rows, turned, outbox, own_a, own_b, next1_a, next1_b, next2_a, next2_b, chosen, level, level1, level2, inverse, total,
    small_sem, load_sem, late_sem, send_sem, recv_sem, fwd_sem, n1_sem, n2_sem, lvl_send, lvl_recv,
):
    me = lax.axis_index("aux")
    occ = lax.axis_index("occ")
    my_x, my_z = me // NZ, me % NZ
    even = occ % 2 == 0

    early = my_z < NZ // 2
    late = jnp.logical_not(early)
    x_at = [lax.rem(my_x + NX - dx, NX) * NZ for dx in range(NX)]
    z_at = [lax.rem(my_z + NZ - dz, NZ // 2) for dz in range(NZ // 2)]

    def behind(side, j):
        dx, dz = OFFSETS[j]
        return x_at[dx] + side * (NZ // 2) + z_at[dz]

    def at_occ(step):
        return (me, (occ + step + N_OCC) % N_OCC)

    def load(part, third):
        s = third * 4
        return pltpu.make_async_copy(
            ints_ref.at[pl.ds(s, 4), pl.ds(part * HALF, HALF)],
            raw.at[pl.ds(s, 4), pl.ds(part * HALF, HALF)],
            load_sem.at[part, third],
        )

    small = [
        pltpu.make_async_copy(src, dst, small_sem.at[i])
        for i, (src, dst) in enumerate((
            (coef_hbm, coef_ref), (tiles_hbm, tiles_ref), (pairs_hbm, pairs_ref),
            (occ_hbm, occ_ref), (virt_hbm, virt_ref),
        ))
    ]
    for copy in small:
        copy.start()
    for part in range(PARTS):
        for third in range(3):
            load(part, third).start()

    barrier = pltpu.get_barrier_semaphore()

    def greet(side, start):
        for j in range(start, SIDE):
            pl.semaphore_signal(barrier, inc=1, device_id=(behind(side, j), occ), device_id_type=MESH)

    @pl.when(early)
    def _():
        greet(0, 1)
        greet(1, 0)

    @pl.when(late)
    def _():
        greet(1, 1)

    for step in (1, 2, -1, -2):
        pl.semaphore_signal(barrier, inc=1, device_id=at_occ(step), device_id_type=MESH)

    for copy in small:
        copy.wait()

    coef = coef_ref[...]
    lane = lax.broadcasted_iota(jnp.int32, (WIDTH, 128), 1) % MP
    row = lax.broadcasted_iota(jnp.int32, (WIDTH, 128), 0)
    slot_of = lax.broadcasted_iota(jnp.int32, (1, DEPTH), 1) // MP
    pairs = pairs_ref[...]
    first = jnp.full((1, DEPTH), -1, jnp.int32)
    second = jnp.full((1, DEPTH), -1, jnp.int32)
    for s in range(NPT):
        first = jnp.where(slot_of == s, pairs[0:1, s : s + 1], first)
        second = jnp.where(slot_of == s, pairs[1:2, s : s + 1], second)
    tiles = tiles_ref[...]
    diagonal = lax.broadcasted_iota(jnp.int32, (N_AUX, N_AUX), 0) == lax.broadcasted_iota(
        jnp.int32, (N_AUX, N_AUX), 1
    )
    tile_of = [
        jnp.sum(jnp.where(diagonal, tiles[d : d + 1, :], 0), axis=1, keepdims=True) for d in range(DT)
    ]
    for parity in range(2):
        picked = jnp.zeros((N_AUX, DEPTH), f32)
        for d in range(DT):
            spread = (row == d * TILE + 2 * lane + parity).astype(f32).astype(bf16)
            values = jnp.dot(coef, spread, preferred_element_type=f32)
            values = jnp.concatenate([values] * (DEPTH // 128), axis=1)
            picked = jnp.where(tile_of[d] == first, values, picked)
        for d in range(DT):
            part_rows = jnp.where(tile_of[d] == second, picked, 0.0)
            start = parity * 128 + (d % 2) * 64 + (d // 2) * 32
            chosen[start : start + 32, :] = part_rows.astype(bf16)

    virt = virt_ref[...].astype(f32)
    tile_row = lax.broadcasted_iota(jnp.int32, (NBT, TILE), 0)
    mine = lax.broadcasted_iota(jnp.int32, (1, N_AUX), 1) == me
    pieces = []
    for d in range(DT):
        tile = jnp.sum(jnp.where(mine, tiles[d : d + 1, :], 0), axis=1, keepdims=True)
        pieces.append(jnp.sum(jnp.where(tile_row == tile, virt, 0.0), axis=0, keepdims=True))
    domain = jnp.concatenate(pieces, axis=1)
    occupied = jnp.sum(jnp.where(mine, occ_ref[...].astype(f32), 0.0), axis=1, keepdims=True)
    level[...] = jnp.broadcast_to(occupied - domain, (8, WIDTH))

    low_half = lax.broadcasted_iota(jnp.int32, (64, 128), 1) < TILE

    def transform(part):
        for third in range(3):
            load(part, third).wait()

        def spread_rows(s, carry):
            for mp in range(MP):
                base = (s * MP + mp) * PITCH
                rows[pl.ds(base, HALF), :] = raw[
                    s, part * HALF : (part + 1) * HALF, mp * 128 : (mp + 1) * 128
                ].astype(f32)
            return carry

        lax.fori_loop(0, NPT, spread_rows, 0)
        matrix = chosen[...]
        for p in range(0, HALF, 2):
            panel = jnp.concatenate(
                [rows[pl.ds(p + i, DEPTH, stride=PITCH), :].astype(bf16) for i in range(2)], axis=1
            )
            product = jnp.dot(matrix, panel, preferred_element_type=f32)
            for i in range(2):
                c = slice(i * 128, (i + 1) * 128)
                straight = jnp.where(low_half, product[0:64, c], product[192:256, c])
                crossed = jnp.where(low_half, product[64:128, c], product[128:192, c])
                turned[(p + i) * TURN : (p + i) * TURN + 64, :] = straight + pltpu.roll(crossed, TILE, 1)
        for r in range(N_AUX):
            for pair in range(2):
                block = turned[pl.ds(pair * 32 + r, HALF, stride=TURN), :]
                outbox[
                    r, part * HALF : (part + 1) * HALF, pair * 128 : (pair + 1) * 128
                ] = block.astype(bf16)

    def send(side, same, part, js=range(SIDE)):
        for j in js:
            to = behind(side, j)
            if part is None:
                src, dst, sem = outbox.at[to], own_a.at[j], recv_sem.at[j // BUNCH]
            else:
                src, dst = outbox.at[to, pl.ds(part * HALF, HALF)], own_b.at[part, j]
                sem = recv_sem.at[N_FIRST * (1 + part) + j // BUNCH]
            if same and j == 0:
                pltpu.make_async_copy(src, dst, sem).start()
            else:
                pltpu.make_async_remote_copy(
                    src_ref=src, dst_ref=dst, send_sem=send_sem, recv_sem=sem,
                    device_id=(to, occ), device_id_type=MESH,
                ).start()

    def pass_level(step, target):
        return pltpu.make_async_remote_copy(
            src_ref=level, dst_ref=target, send_sem=lvl_send.at[step - 1], recv_sem=lvl_recv.at[step - 1],
            device_id=at_occ(step), device_id_type=MESH,
        )

    own, next1, next2 = (own_a, own_b), (next1_a, next1_b), (next2_a, next2_b)

    def bunch(refs, i):
        which, part, j = BUNCHES[i]
        if which == 0:
            return refs[0].at[pl.ds(j, BUNCH)]
        return refs[1].at[part, pl.ds(j, BUNCH)]

    def to_next(i):
        return pltpu.make_async_remote_copy(
            src_ref=bunch(own, i), dst_ref=bunch(next1, i), send_sem=fwd_sem.at[0], recv_sem=n1_sem.at[i],
            device_id=at_occ(1), device_id_type=MESH,
        )

    def to_second(i):
        return pltpu.make_async_remote_copy(
            src_ref=bunch(own, i), dst_ref=bunch(next2, i), send_sem=fwd_sem.at[1], recv_sem=n2_sem.at[i],
            device_id=at_occ(2), device_id_type=MESH,
        )

    def relay(i):
        return pltpu.make_async_remote_copy(
            src_ref=bunch(next1, i), dst_ref=bunch(next2, i), send_sem=fwd_sem.at[2], recv_sem=n2_sem.at[i],
            device_id=at_occ(1), device_id_type=MESH,
        )

    def drain(ref, sem):
        pltpu.make_async_remote_copy(
            src_ref=ref, dst_ref=ref, send_sem=sem, recv_sem=recv_sem.at[0],
            device_id=at_occ(1), device_id_type=MESH,
        ).wait_send()

    def take_own(i, direct):
        came = bunch(own, i)
        pltpu.make_async_remote_copy(
            src_ref=came, dst_ref=came, send_sem=send_sem, recv_sem=recv_sem.at[i],
            device_id=at_occ(1), device_id_type=MESH,
        ).wait_recv()
        if i in direct:
            to_second(i).start()
        else:

            @pl.when(even)
            def _():
                to_second(i).start()

        to_next(i).start()

    def take_next(i, direct):
        to_next(i).wait_recv()
        if i not in direct:

            @pl.when(even)
            def _():
                relay(i).start()

    def take_second(i):
        to_second(i).wait_recv()

    def send_late(i):
        part, first_j = divmod(i * BUNCH, SIDE)
        send(1, True, part, range(first_j, first_j + BUNCH))

    transform(0)

    @pl.when(early)
    def _():
        transform(1)

    pl.semaphore_wait(barrier, jnp.where(early, SIDE - 1 + 4, N_AUX - 1 + 4))

    @pl.when(early)
    def _():
        send(0, True, None)

    @pl.when(late)
    def _():
        for j in range(SIDE):
            pl.semaphore_signal(late_sem, inc=1, device_id=(behind(0, j), occ), device_id_type=MESH)
        send(0, False, 0)
        transform(1)
        send(0, False, 1)
        for i in range(AHEAD):
            send_late(i)

    pass_level(1, level1).start()
    pass_level(2, level2).start()

    def multiply(g, refs, which, part, fresh):
        left, right = own[which], refs[which]
        if which == 0:
            left, right = left[...], right[...]
        else:
            left, right = left[part], right[part]
        depth = left.shape[0] * left.shape[1]
        product = lax.dot_general(
            left.reshape(depth, WIDTH), right.reshape(depth, WIDTH),
            (((0,), (0,)), ((), ())), preferred_element_type=f32,
        )
        total[g] = product if fresh else total[g] + product

    def finish(g):
        value = total[g]
        ratio = value * inverse[g]
        amp_ref[g] = ratio.astype(bf16)
        energy_ref[0, g] = jnp.sum(ratio * value) / (WIDTH * WIDTH)

    def energies():
        pass_level(1, level1).wait()
        pass_level(2, level2).wait()
        column = jnp.transpose(jnp.broadcast_to(level[0:1, :], (WIDTH, WIDTH)))
        for g, other in enumerate((level, level1, level2)):
            inverse[g] = 1.0 / (column + other[0:1, :])

    def pipeline(order, direct, hook):
        count = {}

        def advance(g, refs, i):
            which, part, _ = BUNCHES[i]
            key = (g, which, part)
            count[key] = count.get(key, 0) + 1
            if count[key] == N_FIRST:
                fresh = not any(k[0] == g and k != key and n == N_FIRST for k, n in count.items())
                multiply(g, refs, which, part, fresh)

        n = N_BUNCH
        for step in range(n):
            take_own(order[step], direct)
            hook(step)
            if step >= LAG:
                take_next(order[step - LAG], direct)
            if step >= LAG2:
                take_second(order[step - LAG2])
            if step == n - 1:
                for back in range(LAG - 1, 0, -1):
                    take_next(order[n - 1 - back], direct)
            advance(0, own, order[step])
            if step >= LAG:
                advance(1, next1, order[step - LAG])
            if step >= LAG2:
                advance(2, next2, order[step - LAG2])
            if step == LAG2:
                energies()
        finish(0)
        take_next(order[n - 1], direct)
        for back in range(LAG - 1, -1, -1):
            advance(1, next1, order[n - 1 - back])
        finish(1)
        for back in range(LAG2 - 1, -1, -1):
            take_second(order[n - 1 - back])
            advance(2, next2, order[n - 1 - back])
        finish(2)
        drain(outbox.at[pl.ds(0, N_AUX - 1)], send_sem)
        drain(own_a, fwd_sem.at[0])
        drain(own_b, fwd_sem.at[0])

        @pl.when(even)
        def _():
            drain(own_a, fwd_sem.at[1])
            drain(own_b, fwd_sem.at[1])
            for i in order:
                if i not in direct:
                    drain(bunch(own, i), fwd_sem.at[2])

        @pl.when(jnp.logical_not(even))
        def _():
            for i in direct:
                drain(bunch(own, i), fwd_sem.at[1])

    @pl.when(early)
    def _():
        def hook(step):
            if step == ANSWER:
                pl.semaphore_wait(late_sem, SIDE)
            start = (step - ANSWER) * PACE
            if 0 <= start < SIDE:
                send(1, False, None, range(start, start + PACE))

        pipeline(*EARLY, hook)

    @pl.when(late)
    def _():
        def hook(step):
            if step + AHEAD < PARTS * N_FIRST:
                send_late(step + AHEAD)

        pipeline(*LATE, hook)


def per_device(integrals, tile_pairs, orbital_coef, domains, occ_energy, virt_energy):
    vmem = pl.BlockSpec(memory_space=pltpu.VMEM)
    smem = pl.BlockSpec(memory_space=pltpu.SMEM)
    amps, energies = pl.pallas_call(
        kernel,
        out_shape=(
            jax.ShapeDtypeStruct((STEPS + 1, WIDTH, WIDTH), bf16),
            jax.ShapeDtypeStruct((1, STEPS + 1), f32),
        ),
        in_specs=[pl.BlockSpec(memory_space=pltpu.HBM)] * 6,
        out_specs=(vmem, smem),
        scratch_shapes=[
            pltpu.VMEM((2, NPT), jnp.int32),
            pltpu.VMEM((N_AUX, WIDTH), bf16),
            pltpu.VMEM((DT, N_AUX), jnp.int32),
            pltpu.VMEM((1, N_AUX), bf16),
            pltpu.VMEM((NBT, TILE), bf16),
            pltpu.VMEM((NPT, AUX_DEV, TILE * TILE), bf16),
            pltpu.VMEM((DEPTH * PITCH, 128), f32),
            pltpu.VMEM((HALF * TURN, 128), f32),
            pltpu.VMEM((N_AUX, AUX_DEV, WIDTH), bf16),
            pltpu.VMEM((SIDE, AUX_DEV, WIDTH), bf16),
            pltpu.VMEM((PARTS, SIDE, HALF, WIDTH), bf16),
            pltpu.VMEM((SIDE, AUX_DEV, WIDTH), bf16),
            pltpu.VMEM((PARTS, SIDE, HALF, WIDTH), bf16),
            pltpu.VMEM((SIDE, AUX_DEV, WIDTH), bf16),
            pltpu.VMEM((PARTS, SIDE, HALF, WIDTH), bf16),
            pltpu.VMEM((256, DEPTH), bf16),
            pltpu.VMEM((8, WIDTH), f32),
            pltpu.VMEM((8, WIDTH), f32),
            pltpu.VMEM((8, WIDTH), f32),
            pltpu.VMEM((STEPS + 1, WIDTH, WIDTH), f32),
            pltpu.VMEM((STEPS + 1, WIDTH, WIDTH), f32),
            pltpu.SemaphoreType.DMA((5,)),
            pltpu.SemaphoreType.DMA((PARTS, 3)),
            pltpu.SemaphoreType.REGULAR,
            pltpu.SemaphoreType.DMA,
            pltpu.SemaphoreType.DMA((N_BUNCH,)),
            pltpu.SemaphoreType.DMA((3,)),
            pltpu.SemaphoreType.DMA((N_BUNCH,)),
            pltpu.SemaphoreType.DMA((N_BUNCH,)),
            pltpu.SemaphoreType.DMA((2,)),
            pltpu.SemaphoreType.DMA((2,)),
        ],
        compiler_params=pltpu.CompilerParams(
            collective_id=0, has_side_effects=True, vmem_limit_bytes=40 << 20
        ),
    )(
        *[
            pltpu.with_memory_space_constraint(value, pltpu.HBM)
            for value in (
                integrals,
                tile_pairs.reshape(NPT, 2).T,
                orbital_coef.reshape(N_AUX, WIDTH),
                domains.reshape(N_AUX, DT).T,
                occ_energy.T,
                virt_energy,
            )
        ]
    )
    return (
        amps.reshape(1, 1, STEPS + 1, 1, WIDTH, WIDTH),
        energies.reshape(1, 1, STEPS + 1, 1),
    )


def solution(mesh):
    in_specs = (
        P(None, "aux", None),
        P("aux", None, None),
        P(None, "occ", None),
        P(None, "occ", None),
        P(None, "occ"),
        P(),
    )
    out_specs = (P("aux", "occ", None, None, None, None), P("aux", "occ", None, None))
    return jax.shard_map(
        per_device, mesh=mesh, in_specs=in_specs, out_specs=out_specs, check_vma=False
    )
```
